1024 devices in a mesh: dp: 64 (over z, x), expert: 16 (over y, core).
Axes of the slice: x: 4, y: 8, z: 16, core: 2. Of those that a mesh axis runs over, the one named last changes fastest.
Arguments:
- tokens: bfloat16 [8192, 4096], P('dp'), may hold values from -6 to 6
- out_grad: bfloat16 [8192, 4096], P('dp'), may hold values from -6 to 6
- w_in: bfloat16 [16, 6656, 4096], P('expert', 'dp'), may hold values from -0.09375 to 0.09375
- w_out: bfloat16 [16, 6656, 4096], P('expert', 'dp'), may hold values from -0.0546875 to 0.0546875
- gates: float32 [8, 192], P(None, 'dp'), may hold values from 0.1 to 1
- picks: int32 [8, 192], P(None, 'dp'), may hold values from 0 to 127, as said below
- counts: int32 [8, 64], P(None, 'dp'), may hold values from 0 to 3, as said below
Outputs:
- grad_tokens: bfloat16 [8192, 4096], P('dp', 'expert')
- grad_in: bfloat16 [16, 6656, 4096], P('expert', 'dp')
- grad_out: bfloat16 [16, 6656, 4096], P('expert', 'dp')
- grad_gates: float32 [8, 192], P(None, 'dp')
The draws below stay inside these ranges and needn't reach their ends.
Inputs may be any that keep to these rules, and one draw needn't show every extreme that they name: Within each tile of 3 slots of one expert (slots s * 3 to s * 3 + 2, which belong to shard s) the picks are distinct rows of that shard, padded slots included; a token row may be picked by any number of experts. Only the first counts[e, s] slots of a tile are valid; every expert has at least one full tile.
All inputs are finite; a program needn't handle non-finite values.
Results may differ from the reference program's by a relative error of at most 0.02.
Values may be sent and summed in bfloat16 or wider, within the bound.
A program may use at most 32 MiB of HBM per device.

```python
import math
import jax
import jax.numpy as jnp
from jax import lax

D = 4096
H = 13312
SPLIT = 2
TOK_DEV = 128
ROWS_SHARD = 3
EXPERTS = 8
CAP = 192
TOKENS = 8192


def draw_picks(key, part):
    key = jax.random.fold_in(key, 11)
    shard_count = CAP // ROWS_SHARD
    base = jax.random.randint(key, (EXPERTS, shard_count, TOK_DEV), 0, 65536)
    ranked = base * TOK_DEV + jnp.arange(TOK_DEV, dtype=jnp.int32)
    values, chosen = lax.top_k(ranked, ROWS_SHARD)
    return chosen.reshape(EXPERTS, CAP).astype(jnp.int32)


def draw_counts(key, part):
    key = jax.random.fold_in(key, 23)
    shard_count = CAP // ROWS_SHARD
    key_fill, key_full = jax.random.split(key)
    filled = jax.random.randint(key_fill, (EXPERTS, shard_count), 0, ROWS_SHARD + 1)
    full_tile = jax.random.randint(key_full, (EXPERTS,), 0, shard_count)
    shard_ids = jnp.arange(shard_count, dtype=jnp.int32)
    result = jnp.where(shard_ids[None, :] == full_tile[:, None], ROWS_SHARD, filled)
    return result.astype(jnp.int32)


def level_of(rng, extent, shards, smallest, top_value):
    factor_of = 1.0
    for position, blocks in shards:
        steps = jax.random.uniform(jax.random.fold_in(jax.random.fold_in(rng, 6), position), (blocks,), jnp.float32, smallest / len(shards), top_value / len(shards))
        factor_of = factor_of * jnp.repeat(jnp.exp(steps), extent[position] // blocks).reshape((-1,) + (1,) * (len(extent) - 1 - position))
    return factor_of


def noise(key, extent, scale, limit, cuts=(), kind=jnp.bfloat16):
    values = jax.random.normal(key, extent, jnp.float32) * scale
    if len(cuts) > 0:
        values = level_of(key, extent, cuts, -0.22, 0.18) * values
    return jnp.clip(values, min=-limit, max=limit).astype(kind)


def setup_inputs(seed: int = 0) -> dict:
    keys = jax.random.split(jax.random.key(seed), 8)
    return {
        "tokens": noise(keys[0], (TOKENS, D), 1.0, 6.0, ((0, 64),)),
        "out_grad": noise(keys[1], (TOKENS, D), 1.0, 6.0, ((0, 64),)),
        "w_in": noise(keys[2], (EXPERTS * SPLIT, H // SPLIT, D), D ** -0.5, 0.09375, ((0, 16), (1, 64))),
        "w_out": noise(keys[3], (EXPERTS * SPLIT, H // SPLIT, D), H ** -0.5, 0.0546875, ((0, 16), (1, 64))),
        "gates": jnp.clip(jnp.exp(math.log(1.0) - 2.3025851 * jax.random.uniform(keys[4], (EXPERTS, CAP), jnp.float32) ** level_of(keys[4], (EXPERTS, CAP), ((1, 64),), -0.2, 0.2)), 0.1, 1.0),
        "picks": draw_picks(jax.random.fold_in(keys[7], 71), 0),
        "counts": draw_counts(jax.random.fold_in(keys[7], 71), 0),
    }


gelu_coef = 0.7978845608
cubic_coef = 0.044715


def gelu_tanh(value):
    inner = jnp.tanh(gelu_coef * (value + cubic_coef * value * value * value))
    return 0.5 * value * (1.0 + inner)


def gelu_slope(value):
    inner = jnp.tanh(gelu_coef * (value + cubic_coef * value * value * value))
    return 0.5 * (1.0 + inner) + 0.5 * value * (1.0 - inner * inner) * gelu_coef * (1.0 + 3.0 * cubic_coef * value * value)


def reference(tokens, out_grad, w_in, w_out, gates, picks, counts):
    first_all = w_in.reshape(EXPERTS, H, D)
    second_all = w_out.reshape(EXPERTS, H, D)
    slot_ids = jnp.arange(CAP, dtype=jnp.int32)
    shard_of = (slot_ids // ROWS_SHARD).astype(jnp.int32)
    within = (slot_ids % ROWS_SHARD).astype(jnp.int32)
    contract_last = (((1,), (1,)), ((), ()))
    contract_first = (((0,), (0,)), ((), ()))

    def expert_step(running, per_expert):
        first_proj, second_proj, gate_row, pick_row, count_row = per_expert
        row_ids = (shard_of * TOK_DEV + pick_row).astype(jnp.int32)
        is_valid = within < count_row[shard_of]
        weight = jnp.where(is_valid, gate_row, jnp.zeros_like(gate_row))
        token_rows = tokens[row_ids]
        grad_rows = out_grad[row_ids]
        pre_act = lax.dot_general(token_rows, first_proj, contract_last, preferred_element_type=jnp.float32)
        activation = gelu_tanh(pre_act).astype(jnp.bfloat16)
        outputs = jnp.dot(activation, second_proj, preferred_element_type=jnp.float32)
        score = jnp.sum(grad_rows.astype(jnp.float32) * outputs, axis=1)
        score = jnp.where(is_valid, score, jnp.zeros_like(score))
        back_proj = lax.dot_general(grad_rows, second_proj, contract_last, preferred_element_type=jnp.float32)
        d_pre = (back_proj * weight[:, None] * gelu_slope(pre_act)).astype(jnp.bfloat16)
        upstream = (grad_rows.astype(jnp.float32) * weight[:, None]).astype(jnp.bfloat16)
        grad_second = lax.dot_general(activation, upstream, contract_first, preferred_element_type=jnp.float32).astype(jnp.bfloat16)
        grad_first = lax.dot_general(d_pre, token_rows, contract_first, preferred_element_type=jnp.float32).astype(jnp.bfloat16)
        slot_grads = jnp.dot(d_pre, first_proj, preferred_element_type=jnp.float32)
        running = running.at[row_ids].add(slot_grads)
        return running, (grad_first, grad_second, score)

    start_sum = jnp.zeros((TOKENS, D), jnp.float32)
    running, stacked = lax.scan(expert_step, start_sum, (first_all, second_all, gates, picks, counts))
    grad_first_all, grad_second_all, score_all = stacked
    grad_in = grad_first_all.reshape(EXPERTS * SPLIT, H // SPLIT, D)
    grad_out = grad_second_all.reshape(EXPERTS * SPLIT, H // SPLIT, D)
    return (running.astype(jnp.bfloat16), grad_in, grad_out, score_all)
```

```python
import jax
import jax.numpy as jnp
from jax import lax
from jax.experimental import pallas as pl
from jax.experimental.pallas import tpu as pltpu
from jax.sharding import PartitionSpec as P

MESH = pl.DeviceIdType.MESH
f32 = jnp.float32
bf16 = jnp.bfloat16

gelu_coef = 0.7978845608
cubic_coef = 0.044715

NX, NY, NZ = 4, 8, 16
SLOTS = 3
D = 4096
HID = 104


def device(z, x, y, core):
    return (z * NX + x, y * 2 + core)


def iota(shape, dim):
    return lax.broadcasted_iota(jnp.int32, shape, dim)


def kernel(
    tok_hbm, og_hbm, win_hbm, wout_hbm, gates, picks, counts,
    gtok_out, gin_hbm, gout_hbm, ggate_out,
    src, win, wout, rows_buf, full_tok, full_og, wt_own, wt_in,
    part_own, part_send, part_in, fold, red1, sum1, red2, sum2, red3, total,
    score_own, score_in, msg, msg_in, gin, gout,
    local_sem, send_sem, recv_sem,
):
    dp = lax.axis_index("dp")
    ex = lax.axis_index("expert")
    z, x = dp // NX, dp % NX
    y, core = ex // 2, ex % 2
    zh, zl = z // 4, z % 4
    other = 1 - core

    @pl.when(core == 0)
    def _():
        pltpu.make_async_copy(tok_hbm, src, local_sem.at[0]).start()

    @pl.when(core == 1)
    def _():
        pltpu.make_async_copy(og_hbm, src, local_sem.at[0]).start()

    load_in = pltpu.make_async_copy(win_hbm.at[0], win, local_sem.at[1])
    load_out = pltpu.make_async_copy(wout_hbm.at[0], wout, local_sem.at[2])
    load_in.start()
    load_out.start()

    def mod4(v):
        return lax.rem(v + 4, 4)

    def mod16(v):
        return lax.rem(v + 16, 16)

    flip = 2 - 4 * (z % 2)
    near_z = [mod16(z + 1), mod16(z - 1), mod16(z + flip)]
    far_z = [mod4(zh + k) * 4 + zl for k in (1, -1, 2)]
    side_x = [mod4(x + k) for k in (1, -1, 2)]
    sibling = device(z, x, y, other)

    def pick(first, second):
        return first * other + second * core

    def near_dev(k):
        return device(near_z[k], x, y, core)

    stride_devs = [device(far_z[k], x, y, core) for k in range(3)]
    mid_devs = [device(pick(near_z[k], z), pick(x, side_x[k]), y, core) for k in range(3)]
    last_devs = [device(pick(z, near_z[k]), pick(side_x[k], x), y, core) for k in range(3)]
    y_devs = [device(z, x, lax.rem(y + k, NY), core) for k in range(1, NY)]
    i3 = pick(x, zl)
    i2 = pick(zl, x)
    tgt = (1, -1, 2)
    frm = (-1, 1, 2)

    barrier = pltpu.get_barrier_semaphore()
    greet = (
        stride_devs
        + [near_dev(0), near_dev(1), near_dev(2), device(mod16(z - flip), x, y, core)]
        + [device(z, side_x[k], y, core) for k in range(3)]
        + [sibling]
        + y_devs
    )
    for who in greet:
        pl.semaphore_signal(barrier, inc=1, device_id=who, device_id_type=MESH)

    counter = [0]

    def remote(src_ref, dst_ref, who):
        i = counter[0]
        counter[0] += 1
        return pltpu.make_async_remote_copy(
            src_ref=src_ref, dst_ref=dst_ref, send_sem=send_sem.at[i], recv_sem=recv_sem.at[i],
            device_id=who, device_id_type=MESH,
        )

    sent = []

    def go(copy):
        copy.start()
        sent.append(copy)
        return copy

    r48 = iota((48, 128), 0)
    slot48 = r48 >> 4
    p0, p1, p2 = picks[y, 0], picks[y, 1], picks[y, 2]
    pick48 = jnp.where(slot48 == 0, p0, jnp.where(slot48 == 1, p1, p2))
    hit48 = iota((48, 128), 1) == pick48
    chunk48 = r48 & 15
    pltpu.make_async_copy(tok_hbm, src, local_sem.at[0]).wait()
    own = jnp.zeros((48, 256), f32)
    for q in range(16):
        one = jnp.where(hit48 & (chunk48 == q), 1.0, 0.0).astype(bf16)
        own += jnp.dot(one, src[:, q * 256 : (q + 1) * 256], preferred_element_type=f32)
    rows_buf[core, i3, i2, zh] = own.astype(bf16)

    place = x * 16 + zl * 4 + zh
    spot = iota((8, 128), 0) * 128 + iota((8, 128), 1)
    mine = jnp.zeros((8, 128), f32)
    for j in range(SLOTS):
        wj = jnp.where(j < counts[y, 0], gates[y, j], 0.0)
        mine += jnp.where(spot == j * 64 + place, wj, 0.0)
    wt_own[0] = mine

    pl.semaphore_wait(barrier, len(greet))

    def exchange(views, devs, step):
        copies = []
        for k in range(3):
            copies.append(go(remote(views, views, devs[k])))
        small = []
        for k in range(3):
            small.append(go(remote(wt_own.at[step], wt_in.at[step, k], devs[k])))
        return copies, small

    def add_weights(step, small):
        for c in small:
            c.wait_recv()
        wt_own[step + 1] = wt_own[step] + ((wt_in[step, 0] + wt_in[step, 1]) + wt_in[step, 2])

    copies, small = exchange(rows_buf.at[core, i3, i2, zh], stride_devs, 0)
    add_weights(0, small)
    for c in copies:
        c.wait_recv()
    copies, small = exchange(rows_buf.at[core, i3, i2], mid_devs, 1)
    add_weights(1, small)
    for c in copies:
        c.wait_recv()
    copies, small = exchange(rows_buf.at[core, i3], last_devs, 2)
    hand = [go(remote(rows_buf.at[core, i3], rows_buf.at[core, i3], sibling))]
    add_weights(2, small)
    for k in range(3):
        copies[k].wait_recv()
        got = rows_buf.at[core, mod4(i3 + frm[k])]
        hand.append(go(remote(got, got, sibling)))
    for c in hand:
        c.wait_recv()

    qr, qc = iota((256, 256), 0), iota((256, 256), 1)
    turn = jnp.where(((qr >> 4) == (qc & 15)) & ((qr & 15) == (qc >> 4)), 1.0, 0.0).astype(bf16)

    def unfold(g, carry):
        for j in range(SLOTS):
            rows = pl.ds(pl.multiple_of(j * 64 + g * 16, 16), 16)
            tok16 = rows_buf[0, g, :, :, j * 16 : (j + 1) * 16, :].reshape(256, 256)
            og16 = rows_buf[1, :, g, :, j * 16 : (j + 1) * 16, :].reshape(256, 256)
            tok16 = jnp.dot(turn, tok16, preferred_element_type=f32).astype(bf16)
            og16 = jnp.dot(turn, og16, preferred_element_type=f32).astype(bf16)
            for q in range(16):
                full_tok[rows, q * 256 : (q + 1) * 256] = tok16[q * 16 : (q + 1) * 16]
                full_og[rows, q * 256 : (q + 1) * 256] = og16[q * 16 : (q + 1) * 16]
        return carry

    lax.fori_loop(0, 4, unfold, 0)

    load_in.wait()
    load_out.wait()
    contract_last = (((1,), (1,)), ((), ()))
    pre = lax.dot_general(win[...], full_tok[...], contract_last, preferred_element_type=f32)
    back = lax.dot_general(wout[...], full_og[...], contract_last, preferred_element_type=f32)
    wrow = jnp.concatenate([wt_own[3, 0:1, :], wt_own[3, 1:2, 0:64]], axis=1)
    inner = jnp.tanh(gelu_coef * (pre + cubic_coef * pre * pre * pre))
    act = 0.5 * pre * (1.0 + inner)
    slope = 0.5 * (1.0 + inner) + 0.5 * pre * (1.0 - inner * inner) * gelu_coef * (
        1.0 + 3.0 * cubic_coef * pre * pre
    )
    d_pre = back * wrow * slope
    d_low = d_pre.astype(bf16)
    act_low = (act * wrow).astype(bf16)
    srow = jnp.sum(act.astype(bf16).astype(f32) * back, axis=0, keepdims=True)
    scores = jnp.concatenate(
        [srow[:, 0:128], jnp.concatenate([srow[:, 128:192], jnp.zeros((1, 64), f32)], axis=1)], axis=0
    )
    score_own[0] = jnp.concatenate([scores, jnp.zeros((6, 128), f32)], axis=0)
    d_turn = jnp.transpose(d_pre).astype(bf16)

    def part(half, i):
        cols = pl.ds(pl.multiple_of((2 * i + half) * 256, 256), 256)
        return jnp.dot(d_turn, win[:, cols], preferred_element_type=f32)

    for i in range(8):
        part_send[:, i * 256 : (i + 1) * 256] = part(other, i).astype(bf16)
    swap = go(remote(part_send, part_in, sibling))
    swap_score = go(remote(score_own.at[0], score_in.at[0, 0], sibling))
    for i in range(8):
        part_own[:, i * 256 : (i + 1) * 256] = part(core, i)
    swap.wait_recv()

    for pair in range(2):
        for j in range(SLOTS):
            cols = []
            for g in (2 * pair, 2 * pair + 1):
                lo = j * 64 + g * 16
                both = part_own[lo : lo + 16, :] + part_in[lo : lo + 16, :].astype(f32)
                both = both.astype(bf16)
                cols.append(jnp.concatenate([both[:, q * 128 : (q + 1) * 128] for q in range(16)], axis=0))
            out = jnp.dot(turn, jnp.concatenate(cols, axis=1), preferred_element_type=f32).astype(bf16)
            for n in range(2):
                g = 2 * pair + n
                for d in range(4):
                    for h in range(4):
                        b = d * 4 + h
                        fold[pick(g, d), pick(d, g), h, j * 16 : (j + 1) * 16, :] = out[
                            b * 16 : (b + 1) * 16, n * 128 : (n + 1) * 128
                        ]

    def scatter(views, slots, devs, step):
        copies = [go(remote(views[k], slots.at[k], devs[k])) for k in range(3)]
        small = [go(remote(score_own.at[step], score_in.at[step, k], devs[k])) for k in range(3)]
        return copies, small

    def add_scores(step, small):
        for c in small:
            c.wait_recv()
        score_own[step + 1] = score_own[step] + (
            (score_in[step, 0] + score_in[step, 1]) + score_in[step, 2]
        )

    swap_score.wait_recv()
    score_own[1] = score_own[0] + score_in[0, 0]
    copies, small = scatter([fold.at[mod4(i3 + t)] for t in tgt], red1, last_devs, 1)

    def outer(i, carry):
        cols = pl.ds(pl.multiple_of(i * 512, 512), 512)
        gin[:, cols] = jnp.dot(d_low, full_tok[:, cols], preferred_element_type=f32).astype(bf16)
        gout[:, cols] = jnp.dot(act_low, full_og[:, cols], preferred_element_type=f32).astype(bf16)
        return carry

    lax.fori_loop(0, 8, outer, 0)
    store_in = pltpu.make_async_copy(gin, gin_hbm.at[0], local_sem.at[3])
    store_out = pltpu.make_async_copy(gout, gout_hbm.at[0], local_sem.at[4])
    store_in.start()
    store_out.start()

    add_scores(1, small)
    for c in copies:
        c.wait_recv()

    def sum_one(d, carry):
        t = (fold[i3, d].astype(f32) + red1[0, d].astype(f32)) + (
            red1[1, d].astype(f32) + red1[2, d].astype(f32)
        )
        sum1[d] = t.astype(bf16)
        return carry

    lax.fori_loop(0, 4, sum_one, 0)
    copies, small = scatter([sum1.at[mod4(i2 + t)] for t in tgt], red2, mid_devs, 2)
    add_scores(2, small)
    for c in copies:
        c.wait_recv()
    t = (sum1[i2].astype(f32) + red2[0].astype(f32)) + (red2[1].astype(f32) + red2[2].astype(f32))
    sum2[...] = t.astype(bf16)
    copies, small = scatter([sum2.at[mod4(zh + t)] for t in tgt], red3, stride_devs, 3)
    add_scores(3, small)
    for c in copies:
        c.wait_recv()
    total[...] = (sum2[zh].astype(f32) + red3[0].astype(f32)) + (
        red3[1].astype(f32) + red3[2].astype(f32)
    )

    final = score_own[4]
    r8, l8 = iota((8, 128), 0), iota((8, 128), 1)
    score_row = jnp.zeros((8, 128), f32)
    for j in range(SLOTS):
        s = jnp.sum(jnp.where(spot == j * 64 + place, final, 0.0), keepdims=True)
        score_row += jnp.where((r8 == 6) & (l8 == j), s, 0.0)
    for i in range(8):
        msg[i] = score_row
        for j in range(SLOTS):
            msg[i, 2 * j : 2 * j + 2, :] = total[16 * j + 2 * i : 16 * j + 2 * i + 2, :]
    last = [
        go(remote(msg.at[lax.rem(y + k, NY)], msg_in.at[y], y_devs[k - 1])) for k in range(1, NY)
    ]
    msg_in[y] = msg[y]
    for c in last:
        c.wait_recv()

    token = iota((128, 128), 0)
    for h in range(2):
        acc = jnp.zeros((128, 128), f32)
        for e in range(8):
            for j in range(SLOTS):
                acc += jnp.where(token == picks[e, j], msg_in[e, 2 * j + h : 2 * j + h + 1, :], 0.0)
        gtok_out[:, h * 128 : (h + 1) * 128] = acc.astype(bf16)
    for e in range(8):
        row = msg_in[e, 6:7, :]
        ggate_out[e : e + 1, :] = jnp.where(iota((1, 128), 1) < counts[e, 0], row, 0.0)

    for c in sent:
        c.wait_send()
    store_in.wait()
    store_out.wait()


def on_device(tokens, out_grad, w_in, w_out, gates, picks, counts):
    hbm = pl.BlockSpec(memory_space=pl.ANY)
    vmem = pl.BlockSpec(memory_space=pltpu.VMEM)
    smem = pl.BlockSpec(memory_space=pltpu.SMEM)
    sems = pltpu.SemaphoreType.DMA
    g_tok, g_in, g_out, g_gate = pl.pallas_call(
        kernel,
        out_shape=(
            jax.ShapeDtypeStruct((128, 256), bf16),
            jax.ShapeDtypeStruct((1, HID, D), bf16),
            jax.ShapeDtypeStruct((1, HID, D), bf16),
            jax.ShapeDtypeStruct((8, 128), f32),
        ),
        in_specs=[hbm, hbm, hbm, hbm, smem, smem, smem],
        out_specs=(vmem, hbm, hbm, vmem),
        scratch_shapes=[
            pltpu.VMEM((128, D), bf16),
            pltpu.VMEM((HID, D), bf16),
            pltpu.VMEM((HID, D), bf16),
            pltpu.VMEM((2, 4, 4, 4, 48, 256), bf16),
            pltpu.VMEM((192, D), bf16),
            pltpu.VMEM((192, D), bf16),
            pltpu.VMEM((4, 8, 128), f32),
            pltpu.VMEM((3, 3, 8, 128), f32),
            pltpu.VMEM((192, D // 2), f32),
            pltpu.VMEM((192, D // 2), bf16),
            pltpu.VMEM((192, D // 2), bf16),
            pltpu.VMEM((4, 4, 4, 48, 128), bf16),
            pltpu.VMEM((3, 4, 4, 48, 128), bf16),
            pltpu.VMEM((4, 4, 48, 128), bf16),
            pltpu.VMEM((3, 4, 48, 128), bf16),
            pltpu.VMEM((4, 48, 128), bf16),
            pltpu.VMEM((3, 48, 128), bf16),
            pltpu.VMEM((48, 128), f32),
            pltpu.VMEM((5, 8, 128), f32),
            pltpu.VMEM((4, 3, 8, 128), f32),
            pltpu.VMEM((8, 8, 128), f32),
            pltpu.VMEM((8, 8, 128), f32),
            pltpu.VMEM((HID, D), bf16),
            pltpu.VMEM((HID, D), bf16),
            sems((5,)),
            sems((56,)),
            sems((56,)),
        ],
        compiler_params=pltpu.CompilerParams(
            collective_id=0, has_side_effects=True, vmem_limit_bytes=48 * 2**20
        ),
        cost_estimate=pl.CostEstimate(flops=10**9, bytes_accessed=8 * 10**6, transcendentals=20000),
        name="expert_backward",
    )(tokens, out_grad, w_in, w_out, gates, picks, counts)
    return g_tok, g_in, g_out, g_gate[:, :SLOTS]


def solution(mesh):
    placed = (
        P("dp", None),
        P("dp", None),
        P("expert", "dp", None),
        P("expert", "dp", None),
        P(None, "dp"),
        P(None, "dp"),
        P(None, "dp"),
    )
    return jax.shard_map(
        on_device,
        mesh=mesh,
        in_specs=placed,
        out_specs=(
            P("dp", "expert"),
            P("expert", "dp", None),
            P("expert", "dp", None),
            P(None, "dp"),
        ),
        check_vma=False,
    )
```

```python
import jax
import jax.numpy as jnp
from jax import lax
from jax.experimental import pallas as pl
from jax.experimental.pallas import tpu as pltpu
from jax.sharding import PartitionSpec as P

MESH = pl.DeviceIdType.MESH
f32 = jnp.float32
bf16 = jnp.bfloat16

gelu_coef = 0.7978845608
cubic_coef = 0.044715

NX, NY, NZ = 4, 8, 16
SLOTS = 3
D = 4096
HID = 104


def device(z, x, y, core):
    return (z * NX + x, y * 2 + core)


def iota(shape, dim):
    return lax.broadcasted_iota(jnp.int32, shape, dim)


def kernel(
    tok_hbm, og_hbm, win_hbm, wout_hbm, gates, picks, counts,
    msg_out, gate_out, gin_hbm, gout_hbm,
    src, win, wout, rows_buf, full_tok, full_og,
    part_own, part_send, part_in, fold, red1, sum1, red2, sum2,
    score_own, score_in, msg, msg_in, gin, gout,
    local_sem, send_sem, recv_sem,
):
    dp = lax.axis_index("dp")
    ex = lax.axis_index("expert")
    z, x = dp // NX, dp % NX
    y, core = ex // 2, ex % 2
    zh, zl = z // 4, z % 4
    other = 1 - core

    @pl.when(core == 0)
    def _():
        pltpu.make_async_copy(tok_hbm, src, local_sem.at[0]).start()

    @pl.when(core == 1)
    def _():
        pltpu.make_async_copy(og_hbm, src, local_sem.at[0]).start()

    load_in = pltpu.make_async_copy(win_hbm.at[0], win, local_sem.at[1])
    load_out = pltpu.make_async_copy(wout_hbm.at[0], wout, local_sem.at[2])
    load_in.start()
    load_out.start()

    def mod4(v):
        return lax.rem(v + 4, 4)

    def mod16(v):
        return lax.rem(v + 16, 16)

    flip = 2 - 4 * (z % 2)
    near_z = [mod16(z + flip), mod16(z + 1), mod16(z - 1)]
    far_z = [mod4(zh + k) * 4 + zl for k in (2, 1, -1)]
    side_x = [mod4(x + k) for k in (2, 1, -1)]
    sibling = device(z, x, y, other)

    def pick(first, second):
        return first * other + second * core

    def near_dev(k):
        return device(near_z[k], x, y, core)

    stride_devs = [device(far_z[k], x, y, core) for k in range(3)]
    mid_devs = [device(pick(near_z[k], z), pick(x, side_x[k]), y, core) for k in range(3)]
    last_devs = [device(pick(z, near_z[k]), pick(side_x[k], x), y, core) for k in range(3)]
    near4 = (0, 1, -1, 2)
    end_devs = [
        [device(mod4(zh + k) * 4 + zl, x, lax.rem(y + m, NY), core) for m in range(NY)] for k in near4
    ]
    i3 = pick(x, zl)
    i2 = pick(zl, x)
    tgt = (2, 1, -1)
    frm = (2, -1, 1)

    barrier = pltpu.get_barrier_semaphore()
    greet = (
        end_devs[0][1:]
        + end_devs[1]
        + end_devs[2]
        + end_devs[3]
        + [near_dev(0), near_dev(1), near_dev(2), device(mod16(z - flip), x, y, core)]
        + [device(z, side_x[k], y, core) for k in range(3)]
        + [sibling]
    )
    for who in greet:
        pl.semaphore_signal(barrier, inc=1, device_id=who, device_id_type=MESH)

    counter = [0]

    def remote(src_ref, dst_ref, who):
        i = counter[0]
        counter[0] += 1
        return pltpu.make_async_remote_copy(
            src_ref=src_ref, dst_ref=dst_ref, send_sem=send_sem.at[i], recv_sem=recv_sem.at[i],
            device_id=who, device_id_type=MESH,
        )

    sent = []

    def go(copy):
        copy.start()
        sent.append(copy)
        return copy

    r48 = iota((48, 128), 0)
    slot48 = r48 >> 4
    p0, p1, p2 = picks[0, y], picks[1, y], picks[2, y]
    pick48 = jnp.where(slot48 == 0, p0, jnp.where(slot48 == 1, p1, p2))
    hit48 = iota((48, 128), 1) == pick48
    chunk48 = r48 & 15
    pltpu.make_async_copy(tok_hbm, src, local_sem.at[0]).wait()
    ones = [jnp.where(hit48 & (chunk48 == q), 1.0, 0.0).astype(bf16) for q in range(16)]
    tall = jnp.concatenate([src[:, q * 256 : (q + 1) * 256] for q in range(16)], axis=0)
    own = jnp.dot(jnp.concatenate(ones, axis=1), tall, preferred_element_type=f32)
    slot_col = iota((48, 1), 0) >> 4
    scale = jnp.zeros((48, 1), f32)
    for j in range(SLOTS):
        wj = jnp.where(j < counts[0, y], gates[j, y], 0.0)
        scale = jnp.where(slot_col == j, wj, scale)
    scale = jnp.where(core == 1, scale, 1.0)
    rows_buf[core, i3, i2, zh] = (own * scale).astype(bf16)

    place = x * 16 + zl * 4 + zh
    spot = iota((8, 128), 0) * 128 + iota((8, 128), 1)

    pl.semaphore_wait(barrier, len(greet))

    def exchange(views, devs):
        return [go(remote(views, views, devs[k])) for k in range(3)]

    def to_sibling(view):
        hand.append(go(remote(view, view, sibling)))

    hand = []
    copies = exchange(rows_buf.at[core, i3, i2, zh], stride_devs)
    for c in copies:
        c.wait_recv()
    groups = [i2] + [mod4(i2 + frm[k]) for k in (1, 2, 0)]
    copies = exchange(rows_buf.at[core, i3, i2], mid_devs)
    chunks = [exchange(rows_buf.at[core, i3, i2], last_devs)]
    to_sibling(rows_buf.at[core, i3, i2])
    for n, k in enumerate((1, 2, 0)):
        copies[k].wait_recv()
        view = rows_buf.at[core, i3, groups[n + 1]]
        chunks.append(exchange(view, last_devs))
        to_sibling(view)
    for n in range(4):
        for k in (1, 2, 0):
            chunks[n][k].wait_recv()
            to_sibling(rows_buf.at[core, mod4(i3 + frm[k]), groups[n]])
    for c in hand:
        c.wait_recv()

    qr, qc = iota((256, 256), 0), iota((256, 256), 1)
    turn = jnp.where(((qr >> 4) == (qc & 15)) & ((qr & 15) == (qc >> 4)), 1.0, 0.0).astype(bf16)

    def unfold(g, carry):
        for j in range(SLOTS):
            rows = pl.ds(pl.multiple_of(j * 64 + g * 16, 16), 16)
            tok16 = rows_buf[0, g, :, :, j * 16 : (j + 1) * 16, :].reshape(256, 256)
            og16 = rows_buf[1, :, g, :, j * 16 : (j + 1) * 16, :].reshape(256, 256)
            tok16 = jnp.dot(turn, tok16, preferred_element_type=f32).astype(bf16)
            og16 = jnp.dot(turn, og16, preferred_element_type=f32).astype(bf16)
            for q in range(16):
                full_tok[rows, q * 256 : (q + 1) * 256] = tok16[q * 16 : (q + 1) * 16]
                full_og[rows, q * 256 : (q + 1) * 256] = og16[q * 16 : (q + 1) * 16]
        return carry

    lax.fori_loop(0, 4, unfold, 0)

    load_in.wait()
    load_out.wait()
    contract_last = (((1,), (1,)), ((), ()))
    pre = lax.dot_general(win[...], full_tok[...], contract_last, preferred_element_type=f32)
    back = lax.dot_general(wout[...], full_og[...], contract_last, preferred_element_type=f32)
    inner = jnp.tanh(gelu_coef * (pre + cubic_coef * pre * pre * pre))
    act = 0.5 * pre * (1.0 + inner)
    slope = 0.5 * (1.0 + inner) + 0.5 * pre * (1.0 - inner * inner) * gelu_coef * (
        1.0 + 3.0 * cubic_coef * pre * pre
    )
    d_pre = back * slope
    d_low = d_pre.astype(bf16)
    act_low = act.astype(bf16)
    srow = jnp.sum(act_low.astype(f32) * back, axis=0, keepdims=True)
    scores = jnp.concatenate(
        [srow[:, 0:128], jnp.concatenate([srow[:, 128:192], jnp.zeros((1, 64), f32)], axis=1)], axis=0
    )
    score_own[0] = jnp.concatenate([scores, jnp.zeros((6, 128), f32)], axis=0)
    d_turn = jnp.transpose(d_pre).astype(bf16)

    def part(half, i):
        cols = pl.ds(pl.multiple_of((2 * i + half) * 256, 256), 256)
        return jnp.dot(d_turn, win[:, cols], preferred_element_type=f32)

    for i in range(8):
        part_send[:, i * 256 : (i + 1) * 256] = part(other, i).astype(bf16)
    swap = go(remote(part_send, part_in, sibling))
    swap_score = go(remote(score_own.at[0], score_in.at[0, 0], sibling))
    for i in range(8):
        part_own[:, i * 256 : (i + 1) * 256] = part(core, i)
    swap.wait_recv()

    for pair in range(2):
        for j in range(SLOTS):
            cols = []
            for g in (2 * pair, 2 * pair + 1):
                lo = j * 64 + g * 16
                both = part_own[lo : lo + 16, :] + part_in[lo : lo + 16, :].astype(f32)
                both = both.astype(bf16)
                cols.append(jnp.concatenate([both[:, q * 128 : (q + 1) * 128] for q in range(16)], axis=0))
            out = jnp.dot(turn, jnp.concatenate(cols, axis=1), preferred_element_type=f32).astype(bf16)
            for n in range(2):
                g = 2 * pair + n
                for d in range(4):
                    for h in range(4):
                        b = d * 4 + h
                        fold[pick(g, d), pick(d, g), h, j * 16 : (j + 1) * 16, :] = out[
                            b * 16 : (b + 1) * 16, n * 128 : (n + 1) * 128
                        ]

    def scatter(views, slots, devs, step):
        copies = [go(remote(views[k], slots.at[k], devs[k])) for k in range(3)]
        small = [go(remote(score_own.at[step], score_in.at[step, k], devs[k])) for k in range(3)]
        return copies, small

    def add_scores(step, small):
        for c in small:
            c.wait_recv()
        score_own[step + 1] = score_own[step] + (
            (score_in[step, 0] + score_in[step, 1]) + score_in[step, 2]
        )

    swap_score.wait_recv()
    score_own[1] = score_own[0] + score_in[0, 0]
    copies, small = scatter([fold.at[mod4(i3 + t)] for t in tgt], red1, last_devs, 1)

    def outer(i, carry):
        cols = pl.ds(pl.multiple_of(i * 512, 512), 512)
        gin[:, cols] = jnp.dot(d_low, full_tok[:, cols], preferred_element_type=f32).astype(bf16)
        gout[:, cols] = jnp.dot(act_low, full_og[:, cols], preferred_element_type=f32).astype(bf16)
        return carry

    lax.fori_loop(0, 8, outer, 0)
    store_in = pltpu.make_async_copy(gin, gin_hbm.at[0], local_sem.at[3])
    store_out = pltpu.make_async_copy(gout, gout_hbm.at[0], local_sem.at[4])
    store_in.start()
    store_out.start()

    add_scores(1, small)
    for c in copies:
        c.wait_recv()

    def sum_one(d, carry):
        t = (fold[i3, d].astype(f32) + red1[0, d].astype(f32)) + (
            red1[1, d].astype(f32) + red1[2, d].astype(f32)
        )
        sum1[d] = t.astype(bf16)
        return carry

    lax.fori_loop(0, 4, sum_one, 0)
    copies, small = scatter([sum1.at[mod4(i2 + t)] for t in tgt], red2, mid_devs, 2)
    add_scores(2, small)
    for c in copies:
        c.wait_recv()
    sum2[...] = (sum1[i2].astype(f32) + red2[0].astype(f32)) + (
        red2[1].astype(f32) + red2[2].astype(f32)
    )

    for h in range(4):
        for i in range(NY):
            for j in range(SLOTS):
                msg[h, i, 2 * j : 2 * j + 2, :] = sum2[h, 16 * j + 2 * i : 16 * j + 2 * i + 2, :]
            msg[h, i, 6:8, :] = score_own[3, 0:2, :]
    last = []
    for k in (3, 1, 2, 0):
        to_h = mod4(zh + near4[k])
        for m in (4, 3, 5, 2, 6, 1, 7, 0):
            if k + m > 0:
                to_y = lax.rem(y + m, NY)
                last.append(go(remote(msg.at[to_h, to_y], msg_in.at[zh, y], end_devs[k][m])))
    msg_in[zh, y] = msg[zh, y]
    for c in last:
        c.wait_recv()
    got = (msg_in[0] + msg_in[1]) + (msg_in[2] + msg_in[3])
    msg_out[...] = got
    r8, l8 = iota((8, 128), 0), iota((8, 128), 1)
    gate = jnp.zeros((8, 128), f32)
    for j in range(SLOTS):
        line = got[:, 6 + j // 2, :]
        mine = jnp.sum(jnp.where(l8 == (j % 2) * 64 + place, line, 0.0), axis=1, keepdims=True)
        flat = jnp.sum(jnp.where(l8 == r8, mine, 0.0), axis=0, keepdims=True)
        gate += jnp.where(r8 == j, flat, 0.0)
    gate_out[...] = gate

    for c in sent:
        c.wait_send()
    store_in.wait()
    store_out.wait()


def finish(msg_in, gate, gin_in, gout_in, picks, counts, gates, gtok_out, gin_hbm, gout_hbm, ggate_out, stage, sem):
    loads = [
        pltpu.make_async_copy(gin_in.at[0], stage.at[0], sem.at[0]),
        pltpu.make_async_copy(gout_in.at[0], stage.at[1], sem.at[1]),
    ]
    stores = [
        pltpu.make_async_copy(stage.at[0], gin_hbm.at[0], sem.at[2]),
        pltpu.make_async_copy(stage.at[1], gout_hbm.at[0], sem.at[3]),
    ]
    for c in loads:
        c.start()
    for load, store in zip(loads, stores):
        load.wait()
        store.start()
    token = iota((128, 128), 0)
    for h in range(2):
        acc = jnp.zeros((128, 128), f32)
        for e in range(8):
            for j in range(SLOTS):
                acc += jnp.where(token == picks[j, e], msg_in[e, 2 * j + h : 2 * j + h + 1, :], 0.0)
        gtok_out[:, h * 128 : (h + 1) * 128] = acc.astype(bf16)
    ok = iota((SLOTS, 8), 0) < counts[...]
    ggate_out[...] = jnp.where(ok, gate[0:SLOTS, 0:8] / gates[...], 0.0)
    for c in stores:
        c.wait()


def on_device(tokens, out_grad, w_in, w_out, gates, picks, counts):
    hbm = pl.BlockSpec(memory_space=pl.ANY)
    vmem = pl.BlockSpec(memory_space=pltpu.VMEM)
    smem = pl.BlockSpec(memory_space=pltpu.SMEM)
    sems = pltpu.SemaphoreType.DMA
    gates, picks, counts = gates.T, picks.T, counts.T
    received, gate, g_in, g_out = pl.pallas_call(
        kernel,
        out_shape=(
            jax.ShapeDtypeStruct((8, 8, 128), f32),
            jax.ShapeDtypeStruct((8, 128), f32),
            jax.ShapeDtypeStruct((1, HID, D), bf16),
            jax.ShapeDtypeStruct((1, HID, D), bf16),
        ),
        in_specs=[hbm, hbm, hbm, hbm, smem, smem, smem],
        out_specs=(vmem, vmem, hbm, hbm),
        scratch_shapes=[
            pltpu.VMEM((128, D), bf16),
            pltpu.VMEM((HID, D), bf16),
            pltpu.VMEM((HID, D), bf16),
            pltpu.VMEM((2, 4, 4, 4, 48, 256), bf16),
            pltpu.VMEM((192, D), bf16),
            pltpu.VMEM((192, D), bf16),
            pltpu.VMEM((192, D // 2), f32),
            pltpu.VMEM((192, D // 2), bf16),
            pltpu.VMEM((192, D // 2), bf16),
            pltpu.VMEM((4, 4, 4, 48, 128), bf16),
            pltpu.VMEM((3, 4, 4, 48, 128), bf16),
            pltpu.VMEM((4, 4, 48, 128), bf16),
            pltpu.VMEM((3, 4, 48, 128), bf16),
            pltpu.VMEM((4, 48, 128), f32),
            pltpu.VMEM((5, 8, 128), f32),
            pltpu.VMEM((4, 3, 8, 128), f32),
            pltpu.VMEM((4, NY, 8, 128), f32),
            pltpu.VMEM((4, NY, 8, 128), f32),
            pltpu.VMEM((HID, D), bf16),
            pltpu.VMEM((HID, D), bf16),
            sems((5,)),
            sems((96,)),
            sems((96,)),
        ],
        compiler_params=pltpu.CompilerParams(
            collective_id=0, has_side_effects=True, vmem_limit_bytes=60 * 2**20
        ),
        cost_estimate=pl.CostEstimate(flops=10**9, bytes_accessed=8 * 10**6, transcendentals=20000),
        name="expert_backward",
    )(tokens, out_grad, w_in, w_out, gates, picks, counts)
    g_tok, g_in, g_out, g_gate = pl.pallas_call(
        finish,
        out_shape=(
            jax.ShapeDtypeStruct((128, 256), bf16),
            jax.ShapeDtypeStruct((1, HID, D), bf16),
            jax.ShapeDtypeStruct((1, HID, D), bf16),
            jax.ShapeDtypeStruct((SLOTS, 8), f32),
        ),
        in_specs=[vmem, vmem, hbm, hbm, smem, vmem, vmem],
        out_specs=(vmem, hbm, hbm, vmem),
        scratch_shapes=[pltpu.VMEM((2, HID, D), bf16), sems((4,))],
        name="finish",
    )(received, gate, g_in, g_out, picks, counts, gates)
    return g_tok, g_in, g_out, g_gate.T


def solution(mesh):
    placed = (
        P("dp", None),
        P("dp", None),
        P("expert", "dp", None),
        P("expert", "dp", None),
        P(None, "dp"),
        P(None, "dp"),
        P(None, "dp"),
    )
    return jax.shard_map(
        on_device,
        mesh=mesh,
        in_specs=placed,
        out_specs=(
            P("dp", "expert"),
            P("expert", "dp", None),
            P("expert", "dp", None),
            P(None, "dp"),
        ),
        check_vma=False,
    )
```

```python
import jax
import jax.numpy as jnp
from jax import lax
from jax.experimental import pallas as pl
from jax.experimental.pallas import tpu as pltpu
from jax.sharding import PartitionSpec as P

MESH = pl.DeviceIdType.MESH
f32 = jnp.float32
bf16 = jnp.bfloat16

gelu_coef = 0.7978845608
cubic_coef = 0.044715

NX, NY, NZ = 4, 8, 16
SLOTS = 3
D = 4096
HID = 104


def device(z, x, y, core):
    return (z * NX + x, y * 2 + core)


def iota(shape, dim):
    return lax.broadcasted_iota(jnp.int32, shape, dim)


def kernel(
    tok_hbm, og_hbm, win_hbm, wout_hbm, gates, picks, counts,
    gtok_out, gate_out, gin_hbm, gout_hbm,
    src, win, wout, rows_buf, full_tok, full_og,
    part_own, part_send, part_in, fold, red1, sum1, msg2, in2, sum2, msg3, in3,
    score_own, score_in, gin, gout,
    local_sem, send_sem, recv_sem,
):
    dp = lax.axis_index("dp")
    ex = lax.axis_index("expert")
    z, x = dp // NX, dp % NX
    y, core = ex // 2, ex % 2
    zh, zl = z // 4, z % 4
    other = 1 - core

    @pl.when(core == 0)
    def _():
        pltpu.make_async_copy(tok_hbm, src, local_sem.at[0]).start()

    @pl.when(core == 1)
    def _():
        pltpu.make_async_copy(og_hbm, src, local_sem.at[0]).start()

    load_in = pltpu.make_async_copy(win_hbm.at[0], win, local_sem.at[1])
    load_out = pltpu.make_async_copy(wout_hbm.at[0], wout, local_sem.at[2])
    load_in.start()
    load_out.start()

    def mod4(v):
        return lax.rem(v + 4, 4)

    def mod16(v):
        return lax.rem(v + 16, 16)

    flip = 2 - 4 * (z % 2)
    near_z = [mod16(z + flip), mod16(z + 1), mod16(z - 1)]
    far_z = [mod4(zh + k) * 4 + zl for k in (2, 1, -1)]
    side_x = [mod4(x + k) for k in (2, 1, -1)]
    sibling = device(z, x, y, other)

    def pick(first, second):
        return first * other + second * core

    stride_devs = [device(far_z[k], x, y, core) for k in range(3)]
    from_z = [mod16(z - flip), mod16(z + 1), mod16(z - 1)]
    mid_z, mid_x = [pick(near_z[k], z) for k in range(3)], [pick(x, side_x[k]) for k in range(3)]
    mid_devs = [device(mid_z[k], mid_x[k], y, core) for k in range(3)]
    last_devs = [device(pick(z, near_z[k]), pick(side_x[k], x), y, core) for k in range(3)]
    i3 = pick(x, zl)
    i2 = pick(zl, x)
    tgt = (2, 1, -1)
    frm = (2, -1, 1)

    barrier = pltpu.get_barrier_semaphore()
    greet = [device(pick(from_z[k], z), mid_x[k], lax.rem(y + m, NY), core) for m in range(NY) for k in range(3)]
    greet += [device(pick(z, from_z[k]), pick(side_x[k], x), y, core) for k in range(3)]
    greet += stride_devs + [device(z, x, lax.rem(y + m, NY), core) for m in range(1, NY)] + [sibling]
    for who in greet:
        pl.semaphore_signal(barrier, inc=1, device_id=who, device_id_type=MESH)

    counter = [0]

    def remote(src_ref, dst_ref, who):
        i = counter[0]
        counter[0] += 1
        return pltpu.make_async_remote_copy(
            src_ref=src_ref, dst_ref=dst_ref, send_sem=send_sem.at[i], recv_sem=recv_sem.at[i],
            device_id=who, device_id_type=MESH,
        )

    sent = []

    def go(copy):
        copy.start()
        sent.append(copy)
        return copy

    r48 = iota((48, 128), 0)
    slot48 = r48 >> 4
    p0, p1, p2 = picks[0, y], picks[1, y], picks[2, y]
    pick48 = jnp.where(slot48 == 0, p0, jnp.where(slot48 == 1, p1, p2))
    hit48 = iota((48, 128), 1) == pick48
    chunk48 = r48 & 15
    pltpu.make_async_copy(tok_hbm, src, local_sem.at[0]).wait()
    ones = [jnp.where(hit48 & (chunk48 == q), 1.0, 0.0).astype(bf16) for q in range(16)]
    tall = jnp.concatenate([src[:, q * 256 : (q + 1) * 256] for q in range(16)], axis=0)
    own = jnp.dot(jnp.concatenate(ones, axis=1), tall, preferred_element_type=f32)
    slot_col = iota((48, 1), 0) >> 4
    scale = jnp.zeros((48, 1), f32)
    for j in range(SLOTS):
        wj = jnp.where(j < counts[0, y], gates[j, y], 0.0)
        scale = jnp.where(slot_col == j, wj, scale)
    scale = jnp.where(core == 1, scale, 1.0)
    rows_buf[core, i3, i2, zh] = (own * scale).astype(bf16)

    place = x * 16 + zl * 4 + zh
    spot = iota((8, 128), 0) * 128 + iota((8, 128), 1)

    pl.semaphore_wait(barrier, len(greet))

    def exchange(views, devs):
        return [go(remote(views, views, devs[k])) for k in range(3)]

    def to_sibling(view):
        hand.append(go(remote(view, view, sibling)))

    hand = []
    copies = exchange(rows_buf.at[core, i3, i2, zh], stride_devs)
    for c in copies:
        c.wait_recv()
    groups = [i2] + [mod4(i2 + frm[k]) for k in (1, 2, 0)]
    copies = exchange(rows_buf.at[core, i3, i2], mid_devs)
    chunks = [exchange(rows_buf.at[core, i3, i2], last_devs)]
    to_sibling(rows_buf.at[core, i3, i2])
    for n, k in enumerate((1, 2, 0)):
        copies[k].wait_recv()
        view = rows_buf.at[core, i3, groups[n + 1]]
        chunks.append(exchange(view, last_devs))
        to_sibling(view)
    for n in range(4):
        for k in (1, 2, 0):
            chunks[n][k].wait_recv()
            to_sibling(rows_buf.at[core, mod4(i3 + frm[k]), groups[n]])
    for c in hand:
        c.wait_recv()

    qr, qc = iota((256, 256), 0), iota((256, 256), 1)
    turn = jnp.where(((qr >> 4) == (qc & 15)) & ((qr & 15) == (qc >> 4)), 1.0, 0.0).astype(bf16)

    def unfold(g, carry):
        for j in range(SLOTS):
            rows = pl.ds(pl.multiple_of(j * 64 + g * 16, 16), 16)
            tok16 = rows_buf[0, g, :, :, j * 16 : (j + 1) * 16, :].reshape(256, 256)
            og16 = rows_buf[1, :, g, :, j * 16 : (j + 1) * 16, :].reshape(256, 256)
            tok16 = jnp.dot(turn, tok16, preferred_element_type=f32).astype(bf16)
            og16 = jnp.dot(turn, og16, preferred_element_type=f32).astype(bf16)
            for q in range(16):
                full_tok[rows, q * 256 : (q + 1) * 256] = tok16[q * 16 : (q + 1) * 16]
                full_og[rows, q * 256 : (q + 1) * 256] = og16[q * 16 : (q + 1) * 16]
        return carry

    lax.fori_loop(0, 4, unfold, 0)

    load_in.wait()
    load_out.wait()
    contract_last = (((1,), (1,)), ((), ()))
    pre = lax.dot_general(win[...], full_tok[...], contract_last, preferred_element_type=f32)
    back = lax.dot_general(wout[...], full_og[...], contract_last, preferred_element_type=f32)
    inner = jnp.tanh(gelu_coef * (pre + cubic_coef * pre * pre * pre))
    act = 0.5 * pre * (1.0 + inner)
    slope = 0.5 * (1.0 + inner) + 0.5 * pre * (1.0 - inner * inner) * gelu_coef * (
        1.0 + 3.0 * cubic_coef * pre * pre
    )
    d_pre = back * slope
    d_low = d_pre.astype(bf16)
    act_low = act.astype(bf16)
    srow = jnp.sum(act_low.astype(f32) * back, axis=0, keepdims=True)
    scores = jnp.concatenate(
        [srow[:, 0:128], jnp.concatenate([srow[:, 128:192], jnp.zeros((1, 64), f32)], axis=1)], axis=0
    )
    score_own[0] = jnp.concatenate([scores, jnp.zeros((6, 128), f32)], axis=0)
    d_turn = jnp.transpose(d_pre).astype(bf16)

    def part(half, i):
        cols = pl.ds(pl.multiple_of((2 * i + half) * 256, 256), 256)
        return jnp.dot(d_turn, win[:, cols], preferred_element_type=f32)

    for i in range(8):
        part_send[:, i * 256 : (i + 1) * 256] = part(other, i).astype(bf16)
    swap = go(remote(part_send, part_in, sibling))
    swap_score = go(remote(score_own.at[0], score_in.at[0, 0], sibling))
    for i in range(8):
        part_own[:, i * 256 : (i + 1) * 256] = part(core, i)
    swap.wait_recv()

    order = [2 * i + h for h in range(2) for i in range(NY)]
    for pair in range(2):
        for j in range(SLOTS):
            cols = []
            for g in (2 * pair, 2 * pair + 1):
                lo = j * 64 + g * 16
                both = part_own[lo : lo + 16, :] + part_in[lo : lo + 16, :].astype(f32)
                both = both.astype(bf16)
                cols.append(jnp.concatenate([both[:, q * 128 : (q + 1) * 128] for q in order], axis=0))
            out = jnp.dot(turn, jnp.concatenate(cols, axis=1), preferred_element_type=f32).astype(bf16)
            for n in range(2):
                g = 2 * pair + n
                for d in range(4):
                    for h in range(4):
                        b = d * 4 + h
                        fold[pick(g, d), pick(d, g), h, j * 16 : (j + 1) * 16, :] = out[
                            b * 16 : (b + 1) * 16, n * 128 : (n + 1) * 128
                        ]

    def scatter(views, slots, devs, step):
        copies = [go(remote(views[k], slots.at[k], devs[k])) for k in range(3)]
        small = [go(remote(score_own.at[step], score_in.at[step, k], devs[k])) for k in range(3)]
        return copies, small

    def add_scores(step, small):
        for c in small:
            c.wait_recv()
        score_own[step + 1] = score_own[step] + (
            (score_in[step, 0] + score_in[step, 1]) + score_in[step, 2]
        )

    swap_score.wait_recv()
    score_own[1] = score_own[0] + score_in[0, 0]
    copies, small = scatter([fold.at[mod4(i3 + t)] for t in tgt], red1, last_devs, 1)

    def outer(i, carry):
        cols = pl.ds(pl.multiple_of(i * 512, 512), 512)
        gin[:, cols] = jnp.dot(d_low, full_tok[:, cols], preferred_element_type=f32).astype(bf16)
        gout[:, cols] = jnp.dot(act_low, full_og[:, cols], preferred_element_type=f32).astype(bf16)
        return carry

    lax.fori_loop(0, 8, outer, 0)
    store_in = pltpu.make_async_copy(gin, gin_hbm.at[0], local_sem.at[3])
    store_out = pltpu.make_async_copy(gout, gout_hbm.at[0], local_sem.at[4])
    store_in.start()
    store_out.start()

    add_scores(1, small)
    for c in copies:
        c.wait_recv()

    def sum_one(d, carry):
        t = (fold[i3, d].astype(f32) + red1[0, d].astype(f32)) + (
            red1[1, d].astype(f32) + red1[2, d].astype(f32)
        )
        sum1[d] = t
        return carry

    lax.fori_loop(0, 4, sum_one, 0)
    def pack(d, carry):
        lines = score_own[2, 0:2, :]
        for i in range(NY):
            parts = []
            for h in range(4):
                parts.append(sum1[d, h, pl.ds(i, 6, stride=8), :])
                parts.append(lines)
            msg2[d, i] = jnp.concatenate(parts, axis=0).astype(bf16)
        return carry

    lax.fori_loop(0, 4, pack, 0)
    second = []
    for m in (4, 3, 5, 2, 6, 1, 7, 0):
        to_y = lax.rem(y + m, NY)
        for k in range(4):
            if k < 3:
                who = device(mid_z[k], mid_x[k], to_y, core)
                second.append(go(remote(msg2.at[mod4(i2 + tgt[k]), to_y], in2.at[k, y], who)))
            elif m > 0:
                who = device(z, x, to_y, core)
                second.append(go(remote(msg2.at[i2, to_y], in2.at[3, y], who)))
    in2[3, y] = msg2[i2, y]
    for c in second:
        c.wait_recv()
    sum2[...] = (in2[0].astype(f32) + in2[1].astype(f32)) + (in2[2].astype(f32) + in2[3].astype(f32))
    for h in range(4):
        msg3[h] = sum2[:, h * 8 : (h + 1) * 8, :].reshape(64, 128).astype(bf16)
    third = [go(remote(msg3.at[mod4(zh + tgt[k])], in3.at[k], stride_devs[k])) for k in range(3)]
    got = sum2[:, pl.ds(pl.multiple_of(zh * 8, 8), 8), :]
    for c in third:
        c.wait_recv()
    came = (in3[0].astype(f32) + in3[1].astype(f32)) + in3[2].astype(f32)
    got = got + came.reshape(NY, 8, 128)
    token = iota((128, 128), 0)
    for h in range(2):
        acc = jnp.zeros((128, 128), f32)
        for e in range(8):
            for j in range(SLOTS):
                acc += jnp.where(token == picks[j, e], got[e, 2 * j + h : 2 * j + h + 1, :], 0.0)
        gtok_out[:, h * 128 : (h + 1) * 128] = acc.astype(bf16)
    r8, l8 = iota((8, 128), 0), iota((8, 128), 1)
    gate = jnp.zeros((8, 128), f32)
    for j in range(SLOTS):
        line = got[:, 6 + j // 2, :]
        mine = jnp.sum(jnp.where(l8 == (j % 2) * 64 + place, line, 0.0), axis=1, keepdims=True)
        flat = jnp.sum(jnp.where(l8 == r8, mine, 0.0), axis=0, keepdims=True)
        gate += jnp.where(r8 == j, flat, 0.0)
    held, full = jnp.ones((8, 128), f32), jnp.zeros((8, 128), jnp.int32)
    for e in range(8):
        full = jnp.where(l8 == e, counts[0, e], full)
        for j in range(SLOTS):
            held = jnp.where((r8 == j) & (l8 == e), gates[j, e], held)
    gate_out[...] = jnp.where(r8 < full, gate / held, 0.0)

    for c in sent:
        c.wait_send()
    store_in.wait()
    store_out.wait()


def finish(gtok_in, gate, gin_in, gout_in, gtok_hbm, gin_hbm, gout_hbm, ggate_out, sem):
    stores = [
        pltpu.make_async_copy(gin_in, gin_hbm, sem.at[0]),
        pltpu.make_async_copy(gout_in, gout_hbm, sem.at[1]),
        pltpu.make_async_copy(gtok_in, gtok_hbm, sem.at[2]),
    ]
    for c in stores:
        c.start()
    ggate_out[...] = gate[0:SLOTS, 0:8]
    for c in stores:
        c.wait()


def on_device(tokens, out_grad, w_in, w_out, gates, picks, counts):
    hbm = pl.BlockSpec(memory_space=pl.ANY)
    vmem = pl.BlockSpec(memory_space=pltpu.VMEM)
    smem = pl.BlockSpec(memory_space=pltpu.SMEM)
    sems = pltpu.SemaphoreType.DMA
    gates, picks, counts = gates.T, picks.T, counts.T
    g_tok, gate, g_in, g_out = pl.pallas_call(
        kernel,
        out_shape=(
            pltpu.VMEM((128, 256), bf16),
            pltpu.VMEM((8, 128), f32),
            pltpu.VMEM((1, HID, D), bf16),
            pltpu.VMEM((1, HID, D), bf16),
        ),
        in_specs=[hbm, hbm, hbm, hbm, smem, smem, smem],
        out_specs=(vmem, vmem, hbm, hbm),
        scratch_shapes=[
            pltpu.VMEM((128, D), bf16),
            pltpu.VMEM((HID, D), bf16),
            pltpu.VMEM((HID, D), bf16),
            pltpu.VMEM((2, 4, 4, 4, 48, 256), bf16),
            pltpu.VMEM((192, D), bf16),
            pltpu.VMEM((192, D), bf16),
            pltpu.VMEM((192, D // 2), f32),
            pltpu.VMEM((192, D // 2), bf16),
            pltpu.VMEM((192, D // 2), bf16),
            pltpu.VMEM((4, 4, 4, 48, 128), bf16),
            pltpu.VMEM((3, 4, 4, 48, 128), bf16),
            pltpu.VMEM((4, 4, 48, 128), f32),
            pltpu.VMEM((4, NY, 32, 128), bf16),
            pltpu.VMEM((4, NY, 32, 128), bf16),
            pltpu.VMEM((NY, 32, 128), f32),
            pltpu.VMEM((4, 64, 128), bf16),
            pltpu.VMEM((3, 64, 128), bf16),
            pltpu.VMEM((5, 8, 128), f32),
            pltpu.VMEM((4, 3, 8, 128), f32),
            pltpu.VMEM((HID, D), bf16),
            pltpu.VMEM((HID, D), bf16),
            sems((5,)),
            sems((96,)),
            sems((96,)),
        ],
        compiler_params=pltpu.CompilerParams(
            collective_id=0, has_side_effects=True, vmem_limit_bytes=58 * 2**20
        ),
        cost_estimate=pl.CostEstimate(flops=10**9, bytes_accessed=8 * 10**6, transcendentals=20000),
        name="expert_backward",
    )(tokens, out_grad, w_in, w_out, gates, picks, counts)
    g_tok, g_in, g_out, g_gate = pl.pallas_call(
        finish,
        out_shape=(
            jax.ShapeDtypeStruct((128, 256), bf16),
            jax.ShapeDtypeStruct((1, HID, D), bf16),
            jax.ShapeDtypeStruct((1, HID, D), bf16),
            jax.ShapeDtypeStruct((SLOTS, 8), f32),
        ),
        in_specs=[hbm, vmem, hbm, hbm],
        out_specs=(hbm, hbm, hbm, vmem),
        scratch_shapes=[sems((3,))],
        compiler_params=pltpu.CompilerParams(vmem_limit_bytes=6 * 2**20),
        name="finish",
    )(g_tok, gate, g_in, g_out)
    return g_tok, g_in, g_out, g_gate.T


def solution(mesh):
    placed = (
        P("dp", None),
        P("dp", None),
        P("expert", "dp", None),
        P("expert", "dp", None),
        P(None, "dp"),
        P(None, "dp"),
        P(None, "dp"),
    )
    return jax.shard_map(
        on_device,
        mesh=mesh,
        in_specs=placed,
        out_specs=(
            P("dp", "expert"),
            P("expert", "dp", None),
            P("expert", "dp", None),
            P(None, "dp"),
        ),
        check_vma=False,
    )
```
